32 devices in a mesh: slab: 2 (over x), gx: 16 (over z, y, core).
Axes of the slice: x: 2, y: 2, z: 4, core: 2. Of those that a mesh axis runs over, the one named last changes fastest.
Arguments:
- snapshot: float32 [16, 2048, 512], P(None, ('slab', 'gx')), parts along dimension 1, may hold values from -6 to 6
- bitplanes: int32 [32, 8], P(('slab', 'gx')), parts along dimension 0, may hold values from 1 to 15
- slopes: int32 [64], replicated, may hold values from 1 to 536870911, as said below
Outputs:
- coded_values: bfloat16 [16, 2048, 512], P(None, ('slab', 'gx')), parts along dimension 1
- block_distortion: float32 [32, 8], P(('slab', 'gx')), parts along dimension 0
- trial_rates: int32 [12], P('slab'), parts along dimension 0
The draws below stay inside these ranges and needn't reach their ends.
There are 2 independent parts, one for each index of `slab`. The reference program is written for one: setup_inputs(seed, part) draws one part's arguments, and reference() takes and returns one part's arrays. A program takes and returns all parts, laid end to end along the dimension named above; an argument that names none is the same for every part. Nothing has to cross between parts.
Inputs may be any that keep to these rules, and one draw needn't show every extreme that they name: `slopes`: non-decreasing.
All inputs are finite; a program needn't handle non-finite values.
Results may differ from the reference program's by a relative error of at most 0.001.
Values sent between devices are 32-bit elements; how exact they have to be, the bound alone decides.
A program may use at most 64 MiB of HBM per device.

```python
import jax
import jax.numpy as jnp
from jax import lax

NZ = 16
NY = 512
BX = 64
BY = 64
LEVELS = 3
STEPS = 6
CANDS = 64
NX = 1024
NBX = 16
NBY = 8
RATE_TARGET = 256


def draw_bitplanes(key, part):
    key = jax.random.fold_in(key, 7)
    block_x = lax.broadcasted_iota(jnp.int32, (NBX, NBY), 0)
    block_y = lax.broadcasted_iota(jnp.int32, (NBX, NBY), 1)
    ceiling = 5 + 10 * block_x // NBX
    raw_bits = jax.random.randint(key, (NBX, NBY), 0, 1048576)
    planes = raw_bits % ceiling + 1
    planes = jnp.where((block_x == NBX - 1) & (block_y == 0), 15, planes)
    planes = jnp.where((block_x == 0) & (block_y == 0), 1, planes)
    return planes.astype(jnp.int32)


def draw_slopes(key, part):
    key = jax.random.fold_in(key, 11)
    exp_key, off_key = jax.random.split(key)
    positions = jnp.arange(CANDS, dtype=jnp.int32)
    exponent = jax.random.randint(exp_key, (CANDS,), 0, 29)
    base_value = jnp.left_shift(jnp.int32(1), exponent)
    offsets = jax.random.randint(off_key, (CANDS,), 0, 1073741824) % base_value
    values = jnp.sort(base_value + offsets)
    values = jnp.where(positions == 0, 1, values)
    values = jnp.where(positions == CANDS - 1, 536870911, values)
    return values.astype(jnp.int32)


def shard_levels(own_key, shape, pieces, least, top_value):
    gain, own = 1.0, jax.random.fold_in(own_key, 6)
    for dim, parts in pieces:
        steps = jnp.exp(jax.random.uniform(jax.random.fold_in(own, dim), (parts,), jnp.float32, least / len(pieces), top_value / len(pieces)))
        gain = gain * jnp.repeat(steps, shape[dim] // parts).reshape([-1 if axis == dim else 1 for axis in range(len(shape))])
    return gain


def normal_values(own_key, shape, deviation, most, cuts=(), kind=jnp.bfloat16):
    entries = jax.random.normal(own_key, shape, jnp.float32) * deviation
    if len(cuts) > 0:
        entries = shard_levels(own_key, shape, cuts, -0.22, 0.18) * entries
    return jnp.clip(entries, min=-most, max=most).astype(kind)


def setup_inputs(seed: int = 0, part: int = 0) -> dict:
    key_list = jax.random.split(jax.random.key(seed), 4)
    own_keys = jax.random.split(jax.random.fold_in(key_list[3], part), 4)
    snapshot = normal_values(own_keys[0], (NZ, NX, NY), 1.0, 6.0, ((1, 16),), jnp.float32)
    bitplanes = draw_bitplanes(jax.random.fold_in(jax.random.fold_in(key_list[3], part), 71), part)
    slopes = draw_slopes(jax.random.fold_in(key_list[3], 71), part)
    return dict(snapshot=snapshot, bitplanes=bitplanes, slopes=slopes)


ALPHA_LIFT = -1.586134342
BETA_LIFT = -0.05298011854
GAMMA_LIFT = 0.8829110762
DELTA_LIFT = 0.4435068522
KAPPA_SCALE = 1.149604398
QUANT_UNIT = 1.0 / 128.0
LIFT_STEPS = ((ALPHA_LIFT, True), (BETA_LIFT, False), (GAMMA_LIFT, True), (DELTA_LIFT, False))


def odd_rows(values, dim_axis):
    dims = [1, 1, 1]
    dims[dim_axis] = values.shape[dim_axis]
    return (lax.broadcasted_iota(jnp.int32, tuple(dims), dim_axis) % 2) == 1


def periodic_sides(values, dim_axis):
    return jnp.roll(values, 1, dim_axis), jnp.roll(values, -1, dim_axis)


def mirror_sides(values, dim_axis):
    length = values.shape[dim_axis]
    behind = jnp.concatenate([lax.slice_in_dim(values, 1, 2, axis=dim_axis), lax.slice_in_dim(values, 0, length - 1, axis=dim_axis)], dim_axis)
    forward = jnp.concatenate([lax.slice_in_dim(values, 1, length, axis=dim_axis), lax.slice_in_dim(values, length - 2, length - 1, axis=dim_axis)], dim_axis)
    return behind, forward


def lift_axis(values, dim_axis, sides):
    odd_mask = odd_rows(values, dim_axis)
    for coefficient, on_odd in LIFT_STEPS:
        behind, forward = sides(values, dim_axis)
        target = odd_mask if on_odd else jnp.logical_not(odd_mask)
        values = values + jnp.where(target, coefficient * (behind + forward), 0.0)
    return values * jnp.where(odd_mask, 1.0 / KAPPA_SCALE, KAPPA_SCALE)


def kept_planes(bitplanes, trial_slope):
    plane_ids = jnp.arange(1, 16, dtype=jnp.int32)
    powers = jnp.left_shift(jnp.int32(1), 2 * plane_ids)
    hits = (plane_ids[None, None, :] <= bitplanes[:, :, None]) & (powers[None, None, :] >= trial_slope)
    return jnp.sum(hits.astype(jnp.int32), axis=2, dtype=jnp.int32)


def pick_entry(table, index):
    positions = jnp.arange(table.shape[0], dtype=jnp.int32)
    return jnp.sum(jnp.where(positions == index, table, 0), dtype=jnp.int32)


def reference(snapshot, bitplanes, slopes):
    coeffs = snapshot
    for tier_index in range(LEVELS):
        stride = 2 ** tier_index
        subgrid = coeffs[::stride, ::stride, ::stride]
        subgrid = lift_axis(subgrid, 1, periodic_sides)
        subgrid = lift_axis(subgrid, 2, periodic_sides)
        subgrid = lift_axis(subgrid, 0, mirror_sides)
        coeffs = coeffs.at[::stride, ::stride, ::stride].set(subgrid)
    lower = jnp.int32(0)
    upper_end = jnp.int32(CANDS - 1)
    trial_list = []
    for step_index in range(STEPS):
        middle = (lower + upper_end) // 2
        rate_sum = jnp.sum(kept_planes(bitplanes, pick_entry(slopes, middle)), dtype=jnp.int32)
        trial_list.append(rate_sum)
        accept = rate_sum <= RATE_TARGET
        upper_end = jnp.where(accept, middle, upper_end)
        lower = jnp.where(accept, lower, middle + 1)
    kept_final = kept_planes(bitplanes, pick_entry(slopes, lower))
    step_size = QUANT_UNIT * jnp.left_shift(jnp.int32(1), bitplanes - kept_final).astype(jnp.float32)
    step_map = jnp.repeat(jnp.repeat(step_size, BX, axis=0), BY, axis=1)
    magnitude = jnp.abs(coeffs)
    coded_values = (jnp.sign(coeffs) * jnp.maximum(magnitude - step_map, 0.0)).astype(jnp.bfloat16)
    squared_step = step_map * step_map
    ratios = jnp.minimum(coeffs * coeffs, squared_step) / squared_step
    plane_sum = jnp.sum(ratios, axis=0)
    blocks = plane_sum.reshape(bitplanes.shape[0], BX, bitplanes.shape[1], BY).sum(axis=(1, 3)) / (NZ * BX * BY)
    return coded_values, blocks, jnp.stack(trial_list).astype(jnp.int32)
```

```python
import functools

import jax
import jax.numpy as jnp
from jax import lax
from jax.experimental import pallas as pl
from jax.experimental.pallas import tpu as pltpu
from jax.sharding import PartitionSpec as P

NZ, NXL, NY = 16, 64, 512
LANES = 128
NJ = NY // LANES
ROWS = NZ * NXL
CANDS = 64
STEPS = 6
GROUPS = 4

AL = -1.586134342
BE = -0.05298011854
GA = 0.8829110762
DE = 0.4435068522
KA = 1.149604398
QUANT_UNIT = 1.0 / 128.0
MESH = pl.DeviceIdType.MESH


def lane_iota(rows=1):
    return lax.broadcasted_iota(jnp.int32, (rows, LANES), 1)


def y_lift(vals, level):
    s = 2**level
    lane = lane_iota()
    on_even = lane % (2 * s) == 0
    on_odd = lane % (2 * s) == s
    low = lane < s
    high = lane >= LANES - s
    for coefficient, odd in ((AL, True), (BE, False), (GA, True), (DE, False)):
        back = [pltpu.roll(v, s, 1) for v in vals]
        forth = [pltpu.roll(v, LANES - s, 1) for v in vals]
        if odd:
            forth = [jnp.where(high, forth[(j + 1) % NJ], forth[j]) for j in range(NJ)]
        else:
            back = [jnp.where(low, back[(j - 1) % NJ], back[j]) for j in range(NJ)]
        weight = jnp.where(on_odd if odd else on_even, coefficient, 0.0)
        vals = [vals[j] + weight * (back[j] + forth[j]) for j in range(NJ)]
    return vals


def y_scale(level):
    s = 2**level
    lane = lane_iota()
    scale = jnp.where(lane % (2 * s) == 0, KA, 1.0 / KA)
    return jnp.where(lane % s == 0, scale, 1.0), lane % s == 0


def weights(level):
    if level == 0:
        return AL, BE, GA, DE
    own = lane_iota() % 2**level == 0
    return tuple(jnp.where(own, c, 0.0) for c in (AL, BE, GA, DE))


def z_lift(v, level):
    n = len(v)
    w = weights(level)
    v = list(v)
    for coefficient, first in ((w[0], 1), (w[1], 0), (w[2], 1), (w[3], 0)):
        for k in range(first, n, 2):
            a = v[k - 1] if k > 0 else v[k + 1]
            b = v[k + 1] if k < n - 1 else v[k - 1]
            v[k] = v[k] + coefficient * (a + b)
    return v


def shift_up(v, last):
    rows = v.shape[0]
    index = lax.broadcasted_iota(jnp.int32, v.shape, 0)
    return jnp.where(index == rows - 1, last, pltpu.roll(v, rows - 1, 0))


def shift_down(v, first):
    index = lax.broadcasted_iota(jnp.int32, v.shape, 0)
    return jnp.where(index == 0, first, pltpu.roll(v, 1, 0))


def x_lift(even, odd, p, r, e, t, level):
    rows = even.shape[0]
    al, be, ga, de = weights(level)
    d1 = odd + al * (even + shift_up(even, e))
    d1_before = p + al * even[0:1]
    s1 = even + be * (d1 + shift_down(d1, d1_before))
    s1_before = r + be * d1_before
    s1_after = t + be * d1[rows - 1 : rows]
    d2 = d1 + ga * (s1 + shift_up(s1, s1_after))
    d2_before = d1_before + ga * (s1_before + s1[0:1])
    s2 = s1 + de * (d2 + shift_down(d2, d2_before))
    return s2, d2


def kernel(
    n, x_hbm, bits, slopes, coded, dist, trial,
    c0, c1, c2, ob, slope_row, rates,
    sr0, sl0, fl0, fr0, sr1, sl1, fl1, fr1, sr2, sl2, fl2, fr2,
    in_sem, out_sem, rate_send, rate_recv, edge_send, edge_recv,
):
    me = lax.axis_index("gx")
    right, left = lax.rem(me + 1, n), lax.rem(me + n - 1, n)

    group_rows = ROWS // GROUPS
    loads = []
    for g in range(GROUPS):
        for j in range(NJ):
            copy = pltpu.make_async_copy(
                x_hbm.at[pl.ds(g * group_rows, group_rows), pl.ds(j * LANES, LANES)],
                c0.at[j, pl.ds(g * group_rows, group_rows)],
                in_sem.at[g, j],
            )
            copy.start()
            loads.append(copy)

    barrier = pltpu.get_barrier_semaphore()

    def greet(k, carry):
        pl.semaphore_signal(
            barrier, inc=1, device_id={"gx": lax.rem(me + k, n)}, device_id_type=MESH
        )
        return carry

    lax.fori_loop(1, n, greet, 0)

    slope_row[...] = jnp.full((1, LANES), 536870911, jnp.int32)
    slope_row[:, 0:CANDS] = slopes[...]
    trial_slopes = slope_row[...]
    skipped = jnp.zeros((1, LANES), jnp.int32)
    for q in range(1, 16):
        skipped = skipped + jnp.where(trial_slopes > 4**q, 1, 0)
    own = jnp.zeros((1, LANES), jnp.int32)
    for b in range(8):
        own = own + jnp.maximum(bits[0, b] - skipped, 0)
    rates[me] = own

    pl.semaphore_wait(barrier, n - 1)

    def rate_copy(k, row):
        return pltpu.make_async_remote_copy(
            src_ref=rates.at[row],
            dst_ref=rates.at[row],
            send_sem=rate_send.at[k],
            recv_sem=rate_recv.at[k],
            device_id={"gx": lax.rem(me + k, n)},
            device_id_type=MESH,
        )

    def send_rate(k, carry):
        rate_copy(k, me).start()
        return carry

    lax.fori_loop(1, n, send_rate, 0)

    chunk = 32
    levels = (
        (c0, NZ, NXL, sr0, sl0, fl0, fr0),
        (c1, NZ // 2, NXL // 2, sr1, sl1, fl1, fr1),
        (c2, NZ // 4, NXL // 4, sr2, sl2, fl2, fr2),
    )
    for level, (buf, nz, nx, send_right, send_left, from_left, from_right) in enumerate(levels):
        rows = nz * nx

        def y_body(i, carry, buf=buf, level=level):
            at = pl.ds(pl.multiple_of(i * chunk, chunk), chunk)
            vals = y_lift([buf[j, at, :] for j in range(NJ)], level)
            for j in range(NJ):
                buf[j, at, :] = vals[j]
            return carry

        if level == 0:
            for g in range(GROUPS):
                for j in range(NJ):
                    loads[g * NJ + j].wait()
                per = group_rows // chunk
                lax.fori_loop(g * per, (g + 1) * per, y_body, 0)
        else:
            lax.fori_loop(0, rows // chunk, y_body, 0)

        def z_body(i, carry, buf=buf, nz=nz, nx=nx, level=level):
            at = [pl.ds(pl.multiple_of(k * nx + i * 8, 8), 8) for k in range(nz)]
            for j in range(NJ):
                planes = z_lift([buf[j, at[k], :] for k in range(nz)], level)
                for k in range(nz):
                    buf[j, at[k], :] = planes[k]
            return carry

        lax.fori_loop(0, nx // 8, z_body, 0)

        for j in range(NJ):
            def row(x):
                return buf[j, pl.ds(x, nz, stride=nx), :]

            a, b, c, d = row(nx - 4), row(nx - 3), row(nx - 2), row(nx - 1)
            send_right[0, j] = d + AL * c
            send_right[1, j] = c + BE * (b + AL * (a + c))
            a, b, c = row(0), row(1), row(2)
            send_left[0, j] = a
            send_left[1, j] = a + BE * (b + AL * (a + c))
        copies = []
        for side, src, dst, to in (
            (0, send_right, from_left, right),
            (1, send_left, from_right, left),
        ):
            copy = pltpu.make_async_remote_copy(
                src_ref=src,
                dst_ref=dst,
                send_sem=edge_send.at[level, side],
                recv_sem=edge_recv.at[level, side],
                device_id={"gx": to},
                device_id_type=MESH,
            )
            copy.start()
            copies.append(copy)
        for copy in copies:
            copy.wait()

        lanes_scale, lanes_own = y_scale(level)

        def x_body(i, carry, level=level, buf=buf, nz=nz, nx=nx,
                   from_left=from_left, from_right=from_right,
                   lanes_scale=lanes_scale, lanes_own=lanes_own):
            half = nx // 2
            step = 2**level
            for parity in range(2):
                k = 2 * i + parity
                z_gain = 1.0 / KA if parity else KA
                even_scale = jnp.where(lanes_own, lanes_scale * (z_gain * KA), 1.0)
                odd_scale = jnp.where(lanes_own, lanes_scale * (z_gain / KA), 1.0)
                base = k * step * NXL
                for j in range(NJ):
                    even = buf[j, pl.ds(k * nx, half, stride=2), :]
                    odd = buf[j, pl.ds(k * nx + 1, half, stride=2), :]
                    at = pl.ds(k, 1)
                    s2, d2 = x_lift(
                        even, odd, from_left[0, j, at, :], from_left[1, j, at, :],
                        from_right[0, j, at, :], from_right[1, j, at, :], level,
                    )
                    s2 = s2 * even_scale
                    d2 = d2 * odd_scale
                    c0[j, pl.ds(base + step, half, stride=2 * step), :] = d2
                    if parity == 0 and level < 2:
                        to = pl.ds(pl.multiple_of(i * half, 8), half)
                        levels[level + 1][0][j, to, :] = s2
                    else:
                        c0[j, pl.ds(base, half, stride=2 * step), :] = s2
            return carry

        lax.fori_loop(0, nz // 2, x_body, 0)

    def take_rate(k, carry):
        rate_copy(k, lax.rem(me - k + n, n)).wait_recv()
        return carry

    lax.fori_loop(1, n, take_rate, 0)
    total = jnp.sum(rates[...], axis=0)
    lane = lane_iota()
    target = 2 * 8 * n
    total_f = total.astype(jnp.float32)
    over = jnp.where((lane < CANDS - 1) & (total > target), 1.0, 0.0)
    lower = jnp.sum(over).astype(jnp.int32)
    for step in range(STEPS):
        span = 2 ** (STEPS - step)
        middle = (lower // span) * span + span // 2 - 1
        trial[step] = jnp.sum(jnp.where(lane == middle, total_f, 0.0)).astype(jnp.int32)
    skip = jnp.sum(jnp.where(lane == lower, skipped.astype(jnp.float32), 0.0)).astype(jnp.int32)

    step_sizes, squares = [], []
    for j in range(NJ):
        planes = jnp.where(
            lane < 64, jnp.minimum(bits[0, 2 * j], skip), jnp.minimum(bits[0, 2 * j + 1], skip)
        )
        step_sizes.append(QUANT_UNIT * jnp.left_shift(jnp.int32(1), planes).astype(jnp.float32))
        squares.append(jnp.zeros((8, LANES), jnp.float32))

    per = group_rows // chunk
    stores = []
    for g in range(GROUPS):
        def code_body(i, sums):
            at = pl.ds(pl.multiple_of(i * chunk, chunk), chunk)
            out = []
            for j in range(NJ):
                values = c0[j, at, :]
                inside = jnp.clip(values, -step_sizes[j], step_sizes[j])
                ob[at, pl.ds(j * LANES, LANES)] = (values - inside).astype(jnp.bfloat16)
                part = inside * inside
                acc = sums[j]
                for m in range(chunk // 8):
                    acc = acc + part[8 * m : 8 * m + 8]
                out.append(acc)
            return tuple(out)

        squares = lax.fori_loop(g * per, (g + 1) * per, code_body, tuple(squares))
        at = pl.ds(g * group_rows, group_rows)
        copy = pltpu.make_async_copy(ob.at[at], coded.at[at], out_sem.at[g])
        copy.start()
        stores.append(copy)

    result = jnp.zeros((1, 8), jnp.float32)
    column = lax.broadcasted_iota(jnp.int32, (1, 8), 1)
    for j in range(NJ):
        ratio = jnp.sum(squares[j], axis=0, keepdims=True) / (step_sizes[j] * step_sizes[j])
        for half in range(2):
            mine = (lane >= 64) if half else (lane < 64)
            mean = jnp.sum(jnp.where(mine, ratio, 0.0), axis=1, keepdims=True) / (NZ * 64 * 64)
            result = jnp.where(column == 2 * j + half, mean, result)
    dist[...] = result

    def end_rate(k, carry):
        rate_copy(k, me).wait_send()
        return carry

    lax.fori_loop(1, n, end_rate, 0)
    for copy in stores:
        copy.wait()


def body(snapshot, bitplanes, slopes):
    n = lax.axis_size("gx")
    vmem = pl.BlockSpec(memory_space=pltpu.VMEM)
    smem = pl.BlockSpec(memory_space=pltpu.SMEM)
    hbm = pl.BlockSpec(memory_space=pl.ANY)
    edges = []
    for level in range(3):
        edges += [pltpu.VMEM((2, NJ, NZ >> level, LANES), jnp.float32)] * 4
    coded, dist, trial = pl.pallas_call(
        functools.partial(kernel, n),
        out_shape=(
            jax.ShapeDtypeStruct((ROWS, NY), jnp.bfloat16),
            jax.ShapeDtypeStruct((1, 8), jnp.float32),
            jax.ShapeDtypeStruct((STEPS,), jnp.int32),
        ),
        in_specs=[hbm, smem, vmem],
        out_specs=(hbm, vmem, smem),
        scratch_shapes=[
            pltpu.VMEM((NJ, ROWS, LANES), jnp.float32),
            pltpu.VMEM((NJ, ROWS // 4, LANES), jnp.float32),
            pltpu.VMEM((NJ, ROWS // 16, LANES), jnp.float32),
            pltpu.VMEM((ROWS, NY), jnp.bfloat16),
            pltpu.VMEM((1, LANES), jnp.int32),
            pltpu.VMEM((n, 1, LANES), jnp.int32),
            *edges,
            pltpu.SemaphoreType.DMA((GROUPS, NJ)),
            pltpu.SemaphoreType.DMA((GROUPS,)),
            pltpu.SemaphoreType.DMA((n,)),
            pltpu.SemaphoreType.DMA((n,)),
            pltpu.SemaphoreType.DMA((3, 2)),
            pltpu.SemaphoreType.DMA((3, 2)),
        ],
        compiler_params=pltpu.CompilerParams(
            collective_id=0, has_side_effects=True, vmem_limit_bytes=32 * 1024 * 1024
        ),
    )(snapshot.reshape(ROWS, NY), bitplanes, slopes.reshape(1, CANDS))
    return coded.reshape(NZ, NXL, NY), dist, trial


def solution(mesh):
    return jax.shard_map(
        body,
        mesh=mesh,
        in_specs=(P(None, ("slab", "gx"), None), P(("slab", "gx"), None), P()),
        out_specs=(P(None, ("slab", "gx"), None), P(("slab", "gx"), None), P("slab")),
        check_vma=False,
    )
```

```python
import functools

import jax
import jax.numpy as jnp
import ml_dtypes
import numpy as np
from jax import lax
from jax.experimental import pallas as pl
from jax.experimental.pallas import tpu as pltpu
from jax.sharding import PartitionSpec as P

NZ, NXL, NY = 16, 64, 512
LANES = 128
NJ = NY // LANES
ROWS = NZ * NXL
CANDS = 64
STEPS = 6
GROUPS = 4

AL = -1.586134342
BE = -0.05298011854
GA = 0.8829110762
DE = 0.4435068522
KA = 1.149604398
QUANT_UNIT = 1.0 / 128.0
MESH = pl.DeviceIdType.MESH


def lane_iota(rows=1):
    return lax.broadcasted_iota(jnp.int32, (rows, LANES), 1)


def line_lift(get):
    memo = {}

    def state(kind, i):
        if (kind, i) not in memo:
            if kind == "d1":
                v = add(get(i), AL, get(i - 1), get(i + 1))
            elif kind == "s1":
                v = add(get(i), BE, state("d1", i - 1), state("d1", i + 1))
            elif kind == "d2":
                v = add(state("d1", i), GA, state("s1", i - 1), state("s1", i + 1))
            else:
                v = add(state("s1", i), DE, state("d2", i - 1), state("d2", i + 1))
            memo[kind, i] = v
        return memo[kind, i]

    return state


def add(v, weight, a, b):
    if v is None:
        return None
    both = a if b is None else b if a is None else a + b
    return v if both is None else v + weight * both


def crossing(get, before):
    if before:
        inner = add(get(-3), AL, get(-4), get(-2))
        return get(-1) + AL * get(-2), get(-2) + BE * inner
    return get(0), get(0) + BE * add(get(1), AL, get(0), get(2))


def edge_rows(row, keep):
    out, get = [], row
    for level in range(3):
        for before in (True, False):
            if keep(-1 if before else 0):
                out.append((level, before, crossing(get, before)))
        get = next_level(get, keep)
    return out


def next_level(get, keep):
    memo = {}

    def bounded(i):
        if not keep(i):
            return None
        if i not in memo:
            memo[i] = get(i)
        return memo[i]

    state = line_lift(bounded)
    return lambda k: KA * state("s2", 2 * k)


def edge_matrix():
    span = 64
    eye = np.eye(2 * span)

    def row(i):
        return eye[i + span] if -span <= i < span else np.zeros(2 * span)

    behind = edge_rows(row, lambda i: i < 0)
    ahead = edge_rows(row, lambda i: i >= 0)
    true = edge_rows(row, lambda i: True)
    given = np.stack([v for part in (behind, ahead) for _, _, pair in part for v in pair])
    wanted = [v for b in (True, False) for lv, side, pair in true if lv and side == b for v in pair]
    solved = np.linalg.lstsq(given.T, np.stack(wanted).T, rcond=None)[0].T
    assert np.abs(solved @ given - np.stack(wanted)).max() < 1e-9
    return solved


EDGES = edge_matrix()


def y_matrices():
    parts = []
    for level in range(3):
        s = 2**level
        m = np.eye(NY)
        sub = m[:, ::s].copy()
        for coefficient, first in ((AL, 1), (BE, 0), (GA, 1), (DE, 0)):
            sides = np.roll(sub, 1, 1) + np.roll(sub, -1, 1)
            sub[:, first::2] += coefficient * sides[:, first::2]
        sub[:, 0::2] *= KA
        sub[:, 1::2] /= KA
        m[:, ::s] = sub
        m = m[:, LANES : 3 * LANES].astype(np.float32)
        high = m.astype(ml_dtypes.bfloat16)
        low = (m - high.astype(np.float32)).astype(ml_dtypes.bfloat16)
        parts.append(np.stack([high, low]))
    return np.stack(parts)


def y_transform(buf, at, w, level):
    vals = [buf[j, at, :] for j in range(NJ)]
    high = [v.astype(jnp.bfloat16) for v in vals]
    low = [(v - h.astype(jnp.float32)).astype(jnp.bfloat16) for v, h in zip(vals, high)]
    for half in range(2):
        order = [(2 * half - 1) % NJ, 2 * half, 2 * half + 1, (2 * half + 2) % NJ]
        h = jnp.concatenate([high[o] for o in order], axis=1)
        l = jnp.concatenate([low[o] for o in order], axis=1)
        out = (
            jnp.dot(h, w[level, 0], preferred_element_type=jnp.float32)
            + jnp.dot(l, w[level, 0], preferred_element_type=jnp.float32)
            + jnp.dot(h, w[level, 1], preferred_element_type=jnp.float32)
        )
        buf[2 * half, at, :] = out[:, :LANES]
        buf[2 * half + 1, at, :] = out[:, LANES:]


def z_pass(buf, nz, nx, level):
    def z_body(i, carry):
        at = [pl.ds(pl.multiple_of(k * nx + i * 8, 8), 8) for k in range(nz)]
        for j in range(NJ):
            planes = z_lift([buf[j, at[k], :] for k in range(nz)], level)
            for k in range(nz):
                buf[j, at[k], :] = planes[k]
        return carry

    lax.fori_loop(0, nx // 8, z_body, 0)


def weights(level):
    if level == 0:
        return AL, BE, GA, DE
    own = lane_iota() % 2**level == 0
    return tuple(jnp.where(own, c, 0.0) for c in (AL, BE, GA, DE))


def z_lift(v, level):
    n = len(v)
    w = weights(level)
    v = list(v)
    for coefficient, first in ((w[0], 1), (w[1], 0), (w[2], 1), (w[3], 0)):
        for k in range(first, n, 2):
            a = v[k - 1] if k > 0 else v[k + 1]
            b = v[k + 1] if k < n - 1 else v[k - 1]
            v[k] = v[k] + coefficient * (a + b)
    return v


def shift_up(v, last):
    rows = v.shape[0]
    index = lax.broadcasted_iota(jnp.int32, v.shape, 0)
    return jnp.where(index == rows - 1, last, pltpu.roll(v, rows - 1, 0))


def shift_down(v, first):
    index = lax.broadcasted_iota(jnp.int32, v.shape, 0)
    return jnp.where(index == 0, first, pltpu.roll(v, 1, 0))


def x_lift(even, odd, p, r, e, t, level):
    rows = even.shape[0]
    al, be, ga, de = weights(level)
    d1 = odd + al * (even + shift_up(even, e))
    d1_before = p + al * even[0:1]
    s1 = even + be * (d1 + shift_down(d1, d1_before))
    s1_before = r + be * d1_before
    s1_after = t + be * d1[rows - 1 : rows]
    d2 = d1 + ga * (s1 + shift_up(s1, s1_after))
    d2_before = d1_before + ga * (s1_before + s1[0:1])
    s2 = s1 + de * (d2 + shift_down(d2, d2_before))
    return s2, d2


def kernel(
    n, x_hbm, w_hbm, bits_hbm, slopes_hbm, coded, dist, trial,
    c0, c1, c2, h0, h1, h2, w, ob, bits, slopes, slope_row, rates,
    send_right, send_left, from_left, from_right,
    in_sem, w_sem, small_sem, out_sem, rate_send, rate_recv, edge_send, edge_recv,
):
    me = lax.axis_index("gx")
    right, left = lax.rem(me + 1, n), lax.rem(me + n - 1, n)

    group_rows = ROWS // GROUPS
    loads = []
    for g in range(GROUPS):
        for j in range(NJ):
            copy = pltpu.make_async_copy(
                x_hbm.at[pl.ds(g * group_rows, group_rows), pl.ds(j * LANES, LANES)],
                c0.at[j, pl.ds(g * group_rows, group_rows)],
                in_sem.at[g, j],
            )
            copy.start()
            loads.append(copy)
    small = [
        pltpu.make_async_copy(bits_hbm, bits, small_sem.at[0]),
        pltpu.make_async_copy(slopes_hbm, slopes, small_sem.at[1]),
    ]
    w_loads = [pltpu.make_async_copy(w_hbm.at[k], w.at[k], w_sem.at[k]) for k in range(3)]
    for copy in small + w_loads:
        copy.start()

    barrier = pltpu.get_barrier_semaphore()

    def greet(k, carry):
        pl.semaphore_signal(
            barrier, inc=1, device_id={"gx": lax.rem(me + k, n)}, device_id_type=MESH
        )
        return carry

    lax.fori_loop(1, n, greet, 0)

    for copy in loads:
        copy.wait()

    def edge_body(j, carry):
        def row(i):
            return c0[j, pl.ds(i % NXL, NZ, stride=NXL), :]

        for level, _, pair in edge_rows(row, lambda i: i < 0):
            send_right[2 * level, j] = pair[0]
            send_right[2 * level + 1, j] = pair[1]
        for level, _, pair in edge_rows(row, lambda i: i >= 0):
            send_left[2 * level, j] = pair[0]
            send_left[2 * level + 1, j] = pair[1]
        return carry

    lax.fori_loop(0, NJ, edge_body, 0)

    pl.semaphore_wait(barrier, n - 1)
    copies = []
    for side, src, dst, to in (
        (0, send_right, from_left, right),
        (1, send_left, from_right, left),
    ):
        copy = pltpu.make_async_remote_copy(
            src_ref=src,
            dst_ref=dst,
            send_sem=edge_send.at[side],
            recv_sem=edge_recv.at[side],
            device_id={"gx": to},
            device_id_type=MESH,
        )
        copy.start()
        copies.append(copy)

    for copy in small:
        copy.wait()
    slope_row[...] = jnp.full((1, LANES), 536870911, jnp.int32)
    slope_row[:, 0:CANDS] = slopes[...]
    trial_slopes = slope_row[...]
    skipped = jnp.zeros((1, LANES), jnp.int32)
    for q in range(1, 16):
        skipped = skipped + jnp.where(trial_slopes > 4**q, 1, 0)
    own = jnp.zeros((1, LANES), jnp.int32)
    for b in range(8):
        own = own + jnp.maximum(bits[0, b] - skipped, 0)
    rates[me] = own

    def rate_copy(k, row):
        return pltpu.make_async_remote_copy(
            src_ref=rates.at[row],
            dst_ref=rates.at[row],
            send_sem=rate_send.at[k],
            recv_sem=rate_recv.at[k],
            device_id={"gx": lax.rem(me + k, n)},
            device_id_type=MESH,
        )

    def send_rate(k, carry):
        rate_copy(k, me).start()
        return carry

    lax.fori_loop(1, n, send_rate, 0)

    def x_pass(level, buf, nz, nx, nxt, edge, edge_nx, first):
        half = nx // 2
        step = 2**level
        own = lane_iota() % step == 0

        def x_body(i, carry):
            for parity in range(2):
                k = 2 * i + parity
                z_gain = 1.0 / KA if parity else KA
                even_scale, odd_scale = z_gain * KA, z_gain / KA
                if level:
                    even_scale = jnp.where(own, even_scale, 1.0)
                    odd_scale = jnp.where(own, odd_scale, 1.0)
                base = k * step * NXL
                for j in range(NJ):
                    even = buf[j, pl.ds(k * nx, half, stride=2), :]
                    odd = buf[j, pl.ds(k * nx + 1, half, stride=2), :]
                    p, r, e, t = [
                        edge[j, pl.ds(k * edge_nx + first + f, 1), :] for f in range(4)
                    ]
                    s2, d2 = x_lift(even, odd, p, r, e, t, level)
                    s2 = s2 * even_scale
                    d2 = d2 * odd_scale
                    c0[j, pl.ds(base + step, half, stride=2 * step), :] = d2
                    if parity == 0 and level < 2:
                        nxt[j, pl.ds(pl.multiple_of(i * half, 8), half), :] = s2
                    else:
                        c0[j, pl.ds(base, half, stride=2 * step), :] = s2
            return carry

        lax.fori_loop(0, nz // 2, x_body, 0)

    w_loads[0].wait()

    def y_body(i, carry):
        y_transform(c0, pl.ds(pl.multiple_of(i * 256, 256), 256), w, 0)
        return carry

    lax.fori_loop(0, ROWS // 256, y_body, 0)
    z_pass(c0, NZ, NXL, 0)

    for copy in copies:
        copy.wait()

    def cross_body(j, carry):
        mine_right = [send_right[f, j] for f in range(6)]
        mine_left = [send_left[f, j] for f in range(6)]
        theirs_left = [from_left[f, j] for f in range(6)]
        theirs_right = [from_right[f, j] for f in range(6)]

        def put(f, v):
            h0[j, pl.ds(f, NZ, stride=16), :] = v

        put(0, theirs_left[0])
        put(1, theirs_left[1])
        put(2, theirs_right[0])
        put(3, theirs_right[1])
        for f in range(4, 8):
            put(f, jnp.zeros((NZ, LANES), jnp.float32))
        for side, given in ((0, theirs_left + mine_left), (1, mine_right + theirs_right)):
            for f in range(4):
                total = None
                for c, v in zip(EDGES[4 * side + f], given):
                    if abs(c) > 1e-12:
                        total = float(c) * v if total is None else total + float(c) * v
                put(8 + 4 * (f // 2) + 2 * side + f % 2, total)
        return carry

    lax.fori_loop(0, NJ, cross_body, 0)
    y_transform(h0, pl.ds(0, 256), w, 0)
    z_pass(h0, NZ, 16, 0)
    x_pass(0, c0, NZ, NXL, c1, h0, 16, 0)

    w_loads[1].wait()
    for j in range(NJ):
        for k in range(NZ // 2):
            h1[j, pl.ds(8 * k, 8), :] = h0[j, pl.ds(32 * k + 8, 8), :] * KA
    y_transform(c1, pl.ds(0, 256), w, 1)
    z_pass(c1, NZ // 2, NXL // 2, 1)
    y_transform(h1, pl.ds(0, 64), w, 1)
    z_pass(h1, NZ // 2, 8, 1)
    x_pass(1, c1, NZ // 2, NXL // 2, c2, h1, 8, 0)

    w_loads[2].wait()
    for j in range(NJ):
        for k in range(NZ // 4):
            h2[j, pl.ds(8 * k, 8), :] = h1[j, pl.ds(16 * k, 8), :] * KA
    y_transform(c2, pl.ds(0, 64), w, 2)
    z_pass(c2, NZ // 4, NXL // 4, 2)
    y_transform(h2, pl.ds(0, 32), w, 2)
    z_pass(h2, NZ // 4, 8, 2)
    x_pass(2, c2, NZ // 4, NXL // 4, None, h2, 8, 4)

    def take_rate(k, carry):
        rate_copy(k, lax.rem(me - k + n, n)).wait_recv()
        return carry

    lax.fori_loop(1, n, take_rate, 0)
    total = jnp.sum(rates[...], axis=0)
    lane = lane_iota()
    target = 2 * 8 * n
    total_f = total.astype(jnp.float32)
    over = jnp.where((lane < CANDS - 1) & (total > target), 1.0, 0.0)
    lower = jnp.sum(over).astype(jnp.int32)
    for step in range(STEPS):
        span = 2 ** (STEPS - step)
        middle = (lower // span) * span + span // 2 - 1
        trial[step] = jnp.sum(jnp.where(lane == middle, total_f, 0.0)).astype(jnp.int32)
    skip = jnp.sum(jnp.where(lane == lower, skipped.astype(jnp.float32), 0.0)).astype(jnp.int32)

    step_sizes, squares = [], []
    for j in range(NJ):
        planes = jnp.where(
            lane < 64, jnp.minimum(bits[0, 2 * j], skip), jnp.minimum(bits[0, 2 * j + 1], skip)
        )
        step_sizes.append(QUANT_UNIT * jnp.left_shift(jnp.int32(1), planes).astype(jnp.float32))
        squares.append(jnp.zeros((8, LANES), jnp.float32))

    chunk = 32
    per = group_rows // chunk
    stores = []
    for g in range(GROUPS):
        def code_body(i, sums):
            at = pl.ds(pl.multiple_of(i * chunk, chunk), chunk)
            out = []
            for j in range(NJ):
                values = c0[j, at, :]
                inside = jnp.clip(values, -step_sizes[j], step_sizes[j])
                ob[at, pl.ds(j * LANES, LANES)] = (values - inside).astype(jnp.bfloat16)
                part = inside * inside
                acc = sums[j]
                for m in range(chunk // 8):
                    acc = acc + part[8 * m : 8 * m + 8]
                out.append(acc)
            return tuple(out)

        squares = lax.fori_loop(g * per, (g + 1) * per, code_body, tuple(squares))
        at = pl.ds(g * group_rows, group_rows)
        copy = pltpu.make_async_copy(ob.at[at], coded.at[at], out_sem.at[g])
        copy.start()
        stores.append(copy)

    result = jnp.zeros((1, 8), jnp.float32)
    column = lax.broadcasted_iota(jnp.int32, (1, 8), 1)
    for j in range(NJ):
        ratio = jnp.sum(squares[j], axis=0, keepdims=True) / (step_sizes[j] * step_sizes[j])
        for half in range(2):
            mine = (lane >= 64) if half else (lane < 64)
            mean = jnp.sum(jnp.where(mine, ratio, 0.0), axis=1, keepdims=True) / (NZ * 64 * 64)
            result = jnp.where(column == 2 * j + half, mean, result)
    dist[...] = result

    def end_rate(k, carry):
        rate_copy(k, me).wait_send()
        return carry

    lax.fori_loop(1, n, end_rate, 0)
    for copy in stores:
        copy.wait()


def body(snapshot, bitplanes, slopes):
    n = lax.axis_size("gx")
    vmem = pl.BlockSpec(memory_space=pltpu.VMEM)
    smem = pl.BlockSpec(memory_space=pltpu.SMEM)
    hbm = pl.BlockSpec(memory_space=pl.ANY)
    coded, dist, trial = pl.pallas_call(
        functools.partial(kernel, n),
        out_shape=(
            jax.ShapeDtypeStruct((ROWS, NY), jnp.bfloat16),
            jax.ShapeDtypeStruct((1, 8), jnp.float32),
            jax.ShapeDtypeStruct((STEPS,), jnp.int32),
        ),
        in_specs=[hbm, hbm, hbm, hbm],
        out_specs=(hbm, vmem, smem),
        scratch_shapes=[
            pltpu.VMEM((NJ, ROWS, LANES), jnp.float32),
            pltpu.VMEM((NJ, ROWS // 4, LANES), jnp.float32),
            pltpu.VMEM((NJ, ROWS // 16, LANES), jnp.float32),
            pltpu.VMEM((NJ, NZ * 16, LANES), jnp.float32),
            pltpu.VMEM((NJ, NZ // 2 * 8, LANES), jnp.float32),
            pltpu.VMEM((NJ, NZ // 4 * 8, LANES), jnp.float32),
            pltpu.VMEM((3, 2, NY, 2 * LANES), jnp.bfloat16),
            pltpu.VMEM((ROWS, NY), jnp.bfloat16),
            pltpu.SMEM((1, 8), jnp.int32),
            pltpu.VMEM((1, CANDS), jnp.int32),
            pltpu.VMEM((1, LANES), jnp.int32),
            pltpu.VMEM((n, 1, LANES), jnp.int32),
            *[pltpu.VMEM((6, NJ, NZ, LANES), jnp.float32)] * 4,
            pltpu.SemaphoreType.DMA((GROUPS, NJ)),
            pltpu.SemaphoreType.DMA((3,)),
            pltpu.SemaphoreType.DMA((2,)),
            pltpu.SemaphoreType.DMA((GROUPS,)),
            pltpu.SemaphoreType.DMA((n,)),
            pltpu.SemaphoreType.DMA((n,)),
            pltpu.SemaphoreType.DMA((2,)),
            pltpu.SemaphoreType.DMA((2,)),
        ],
        compiler_params=pltpu.CompilerParams(
            collective_id=0, has_side_effects=True, vmem_limit_bytes=60 * 1024 * 1024
        ),
    )(snapshot.reshape(ROWS, NY), jnp.asarray(y_matrices()), bitplanes, slopes.reshape(1, CANDS))
    return coded.reshape(NZ, NXL, NY), dist, trial


def solution(mesh):
    return jax.shard_map(
        body,
        mesh=mesh,
        in_specs=(P(None, ("slab", "gx"), None), P(("slab", "gx"), None), P()),
        out_specs=(P(None, ("slab", "gx"), None), P(("slab", "gx"), None), P("slab")),
        check_vma=False,
    )
```

```python
import functools

import jax
import jax.numpy as jnp
import ml_dtypes
import numpy as np
from jax import lax
from jax.experimental import pallas as pl
from jax.experimental.pallas import tpu as pltpu
from jax.sharding import PartitionSpec as P

NZ, NXL, NY = 16, 64, 512
LANES = 128
NJ = NY // LANES
ROWS = NZ * NXL
CANDS = 64
STEPS = 6
GROUPS = 4

AL = -1.586134342
BE = -0.05298011854
GA = 0.8829110762
DE = 0.4435068522
KA = 1.149604398
QUANT_UNIT = 1.0 / 128.0
MESH = pl.DeviceIdType.MESH


def lane_iota(rows=1):
    return lax.broadcasted_iota(jnp.int32, (rows, LANES), 1)


def line_lift(get):
    memo = {}

    def state(kind, i):
        if (kind, i) not in memo:
            if kind == "d1":
                v = add(get(i), AL, get(i - 1), get(i + 1))
            elif kind == "s1":
                v = add(get(i), BE, state("d1", i - 1), state("d1", i + 1))
            elif kind == "d2":
                v = add(state("d1", i), GA, state("s1", i - 1), state("s1", i + 1))
            else:
                v = add(state("s1", i), DE, state("d2", i - 1), state("d2", i + 1))
            memo[kind, i] = v
        return memo[kind, i]

    return state


def add(v, weight, a, b):
    if v is None:
        return None
    both = a if b is None else b if a is None else a + b
    return v if both is None else v + weight * both


def crossing(get, before):
    if before:
        inner = add(get(-3), AL, get(-4), get(-2))
        return get(-1) + AL * get(-2), get(-2) + BE * inner
    return get(0), get(0) + BE * add(get(1), AL, get(0), get(2))


def edge_rows(row, keep):
    out, get = [], row
    for level in range(3):
        for before in (True, False):
            if keep(-1 if before else 0):
                out.append((level, before, crossing(get, before)))
        get = next_level(get, keep)
    return out


def next_level(get, keep):
    memo = {}

    def bounded(i):
        if not keep(i):
            return None
        if i not in memo:
            memo[i] = get(i)
        return memo[i]

    state = line_lift(bounded)
    return lambda k: KA * state("s2", 2 * k)


def edge_matrix():
    span = 64
    eye = np.eye(2 * span)

    def row(i):
        return eye[i + span] if -span <= i < span else np.zeros(2 * span)

    behind = edge_rows(row, lambda i: i < 0)
    ahead = edge_rows(row, lambda i: i >= 0)
    true = edge_rows(row, lambda i: True)
    given = np.stack([v for part in (behind, ahead) for _, _, pair in part for v in pair])
    wanted = [v for b in (True, False) for lv, side, pair in true if lv and side == b for v in pair]
    solved = np.linalg.lstsq(given.T, np.stack(wanted).T, rcond=None)[0].T
    assert np.abs(solved @ given - np.stack(wanted)).max() < 1e-9
    return solved


EDGES = edge_matrix()


def y_matrices():
    parts = []
    for level in range(3):
        s = 2**level
        m = np.eye(NY)
        sub = m[:, ::s].copy()
        for coefficient, first in ((AL, 1), (BE, 0), (GA, 1), (DE, 0)):
            sides = np.roll(sub, 1, 1) + np.roll(sub, -1, 1)
            sub[:, first::2] += coefficient * sides[:, first::2]
        sub[:, 0::2] *= KA
        sub[:, 1::2] /= KA
        m[:, ::s] = sub
        m = m[:, LANES : 3 * LANES].astype(np.float32)
        high = m.astype(ml_dtypes.bfloat16)
        low = (m - high.astype(np.float32)).astype(ml_dtypes.bfloat16)
        parts.append(np.stack([high, low]))
    return np.stack(parts)


def y_transform(buf, at, w, level):
    vals = [buf[j, at, :] for j in range(NJ)]
    high = [v.astype(jnp.bfloat16) for v in vals]
    low = [(v - h.astype(jnp.float32)).astype(jnp.bfloat16) for v, h in zip(vals, high)]
    rows = vals[0].shape[0]
    orders = [[(2 * half - 1 + m) % NJ for m in range(4)] for half in range(2)]

    def around(parts):
        wide = [jnp.concatenate([parts[o] for o in order], axis=1) for order in orders]
        return jnp.concatenate(wide, axis=0)

    h, l = around(high), around(low)
    out = (
        jnp.dot(h, w[level, 0], preferred_element_type=jnp.float32)
        + jnp.dot(l, w[level, 0], preferred_element_type=jnp.float32)
        + jnp.dot(h, w[level, 1], preferred_element_type=jnp.float32)
    )
    for half in range(2):
        part = out[half * rows : (half + 1) * rows]
        buf[2 * half, at, :] = part[:, :LANES]
        buf[2 * half + 1, at, :] = part[:, LANES:]


def z_pass(buf, nz, nx, level, start=0):
    def z_body(i, carry):
        at = [pl.ds(pl.multiple_of(start + k * nx + i * 8, 8), 8) for k in range(nz)]
        for j in range(NJ):
            planes = z_lift([buf[j, at[k], :] for k in range(nz)], level)
            for k in range(nz):
                buf[j, at[k], :] = planes[k]
        return carry

    lax.fori_loop(0, nx // 8, z_body, 0)


def weights(level):
    if level == 0:
        return AL, BE, GA, DE
    own = lane_iota() % 2**level == 0
    return tuple(jnp.where(own, c, 0.0) for c in (AL, BE, GA, DE))


def z_lift(v, level):
    n = len(v)
    w = weights(level)
    v = list(v)
    for coefficient, first in ((w[0], 1), (w[1], 0), (w[2], 1), (w[3], 0)):
        for k in range(first, n, 2):
            a = v[k - 1] if k > 0 else v[k + 1]
            b = v[k + 1] if k < n - 1 else v[k - 1]
            v[k] = v[k] + coefficient * (a + b)
    return v


def shift_up(v, last):
    rows = v.shape[0]
    index = lax.broadcasted_iota(jnp.int32, v.shape, 0)
    return jnp.where(index == rows - 1, last, pltpu.roll(v, rows - 1, 0))


def shift_down(v, first):
    index = lax.broadcasted_iota(jnp.int32, v.shape, 0)
    return jnp.where(index == 0, first, pltpu.roll(v, 1, 0))


def x_lift(even, odd, p, r, e, t, level):
    rows = even.shape[0]
    al, be, ga, de = weights(level)
    d1 = odd + al * (even + shift_up(even, e))
    d1_before = p + al * even[0:1]
    s1 = even + be * (d1 + shift_down(d1, d1_before))
    s1_before = r + be * d1_before
    s1_after = t + be * d1[rows - 1 : rows]
    d2 = d1 + ga * (s1 + shift_up(s1, s1_after))
    d2_before = d1_before + ga * (s1_before + s1[0:1])
    s2 = s1 + de * (d2 + shift_down(d2, d2_before))
    return s2, d2


def kernel(
    n, x_hbm, w_hbm, bits_hbm, slopes_hbm, c0, info,
    c1, c2, h0, w, bits, slopes, slope_row, rates,
    send_right, send_left, from_left, from_right,
    in_sem, w_sem, small_sem, rate_send, rate_recv, edge_send, edge_recv,
):
    me = lax.axis_index("gx")
    right, left = lax.rem(me + 1, n), lax.rem(me + n - 1, n)

    group_rows = ROWS // GROUPS
    loads = []
    for g in range(GROUPS):
        for j in range(NJ):
            copy = pltpu.make_async_copy(
                x_hbm.at[pl.ds(g * group_rows, group_rows), pl.ds(j * LANES, LANES)],
                c0.at[j, pl.ds(g * group_rows, group_rows)],
                in_sem.at[g, j],
            )
            copy.start()
            loads.append(copy)
    small = [
        pltpu.make_async_copy(bits_hbm, bits, small_sem.at[0]),
        pltpu.make_async_copy(slopes_hbm, slopes, small_sem.at[1]),
    ]
    w_loads = [pltpu.make_async_copy(w_hbm.at[k], w.at[k], w_sem.at[k]) for k in range(3)]
    for copy in small + w_loads:
        copy.start()

    barrier = pltpu.get_barrier_semaphore()

    def greet(k, carry):
        pl.semaphore_signal(
            barrier, inc=1, device_id={"gx": lax.rem(me + k, n)}, device_id_type=MESH
        )
        return carry

    lax.fori_loop(1, n, greet, 0)

    for copy in loads:
        copy.wait()

    def edge_body(j, carry):
        def row(i):
            return c0[j, pl.ds(i % NXL, NZ, stride=NXL), :]

        for level, _, pair in edge_rows(row, lambda i: i < 0):
            send_right[2 * level, j] = pair[0]
            send_right[2 * level + 1, j] = pair[1]
        for level, _, pair in edge_rows(row, lambda i: i >= 0):
            send_left[2 * level, j] = pair[0]
            send_left[2 * level + 1, j] = pair[1]
        return carry

    lax.fori_loop(0, NJ, edge_body, 0)

    pl.semaphore_wait(barrier, n - 1)
    copies = []
    for side, src, dst, to in (
        (0, send_right, from_left, right),
        (1, send_left, from_right, left),
    ):
        copy = pltpu.make_async_remote_copy(
            src_ref=src,
            dst_ref=dst,
            send_sem=edge_send.at[side],
            recv_sem=edge_recv.at[side],
            device_id={"gx": to},
            device_id_type=MESH,
        )
        copy.start()
        copies.append(copy)

    for copy in small:
        copy.wait()
    slope_row[...] = jnp.full((1, LANES), 536870911, jnp.int32)
    slope_row[:, 0:CANDS] = slopes[...]
    trial_slopes = slope_row[...]
    skipped = jnp.zeros((1, LANES), jnp.int32)
    for q in range(1, 16):
        skipped = skipped + jnp.where(trial_slopes > 4**q, 1, 0)
    own = jnp.zeros((1, LANES), jnp.int32)
    for b in range(8):
        own = own + jnp.maximum(bits[0, b] - skipped, 0)
    rates[me] = own

    def rate_copy(k, row):
        return pltpu.make_async_remote_copy(
            src_ref=rates.at[row],
            dst_ref=rates.at[row],
            send_sem=rate_send.at[k],
            recv_sem=rate_recv.at[k],
            device_id={"gx": lax.rem(me + k, n)},
            device_id_type=MESH,
        )

    def send_rate(k, carry):
        rate_copy(k, me).start()
        return carry

    lax.fori_loop(1, n, send_rate, 0)

    def x_pass(level, buf, nz, nx, nxt, edge, edge_nx, first):
        half = nx // 2
        step = 2**level
        own = lane_iota() % step == 0

        def x_body(i, carry):
            for parity in range(2):
                k = 2 * i + parity
                z_gain = 1.0 / KA if parity else KA
                even_scale, odd_scale = z_gain * KA, z_gain / KA
                if level:
                    even_scale = jnp.where(own, even_scale, 1.0)
                    odd_scale = jnp.where(own, odd_scale, 1.0)
                base = k * step * NXL
                for j in range(NJ):
                    even = buf[j, pl.ds(k * nx, half, stride=2), :]
                    odd = buf[j, pl.ds(k * nx + 1, half, stride=2), :]
                    p, r, e, t = [
                        edge[j, pl.ds(first + k * edge_nx + f, 1), :] for f in range(4)
                    ]
                    s2, d2 = x_lift(even, odd, p, r, e, t, level)
                    s2 = s2 * even_scale
                    d2 = d2 * odd_scale
                    c0[j, pl.ds(base + step, half, stride=2 * step), :] = d2
                    if parity == 0 and level < 2:
                        nxt[j, pl.ds(pl.multiple_of(i * half, 8), half), :] = s2
                    else:
                        c0[j, pl.ds(base, half, stride=2 * step), :] = s2
            return carry

        lax.fori_loop(0, nz // 2, x_body, 0)

    w_loads[0].wait()

    def y_body(i, carry):
        y_transform(c0, pl.ds(pl.multiple_of(i * 256, 256), 256), w, 0)
        return carry

    lax.fori_loop(0, ROWS // 256, y_body, 0)
    z_pass(c0, NZ, NXL, 0)

    def take_rate(k, carry):
        rate_copy(k, lax.rem(me - k + n, n)).wait_recv()
        return carry

    lax.fori_loop(1, n, take_rate, 0)
    total = jnp.sum(rates[...], axis=0)
    lane = lane_iota()
    target = 2 * 8 * n
    total_f = total.astype(jnp.float32)
    over = jnp.where((lane < CANDS - 1) & (total > target), 1.0, 0.0)
    lower = jnp.sum(over, axis=1, keepdims=True).astype(jnp.int32)
    found = jnp.zeros((1, LANES), jnp.float32)
    for step in range(STEPS):
        span = 2 ** (STEPS - step)
        middle = (lower & (64 - span)) + (span // 2 - 1)
        picked = jnp.sum(jnp.where(lane == middle, total_f, 0.0), axis=1, keepdims=True)
        found = jnp.where(lane == step, picked, found)
    skip = jnp.sum(
        jnp.where(lane == lower, skipped.astype(jnp.float32), 0.0), axis=1, keepdims=True
    ).astype(jnp.int32)
    for j in range(NJ):
        planes = jnp.minimum(jnp.where(lane < 64, bits[0, 2 * j], bits[0, 2 * j + 1]), skip)
        info[j : j + 1] = QUANT_UNIT * jnp.left_shift(jnp.int32(1), planes).astype(jnp.float32)
    info[4:5] = found

    for copy in copies:
        copy.wait()

    def cross_body(j, carry):
        mine_right = [send_right[f, j] for f in range(6)]
        mine_left = [send_left[f, j] for f in range(6)]
        theirs_left = [from_left[f, j] for f in range(6)]
        theirs_right = [from_right[f, j] for f in range(6)]

        def put(f, v):
            h0[j, pl.ds(f, NZ, stride=16), :] = v

        put(0, theirs_left[0])
        put(1, theirs_left[1])
        put(2, theirs_right[0])
        put(3, theirs_right[1])
        for f in range(4, 8):
            put(f, jnp.zeros((NZ, LANES), jnp.float32))
        for side, given in ((0, theirs_left + mine_left), (1, mine_right + theirs_right)):
            for f in range(4):
                total = None
                for c, v in zip(EDGES[4 * side + f], given):
                    if abs(c) > 1e-12:
                        total = float(c) * v if total is None else total + float(c) * v
                put(8 + 4 * (f // 2) + 2 * side + f % 2, total)
        return carry

    lax.fori_loop(0, NJ, cross_body, 0)
    y_transform(h0, pl.ds(0, 256), w, 0)
    z_pass(h0, NZ, 16, 0)
    x_pass(0, c0, NZ, NXL, c1, h0, 16, 0)

    w_loads[1].wait()
    top = ROWS // 4
    for j in range(NJ):
        for k in range(NZ // 2):
            c1[j, pl.ds(top + 8 * k, 8), :] = h0[j, pl.ds(32 * k + 8, 8), :] * KA
    y_transform(c1, pl.ds(0, top + 64), w, 1)
    z_pass(c1, NZ // 2, NXL // 2, 1)
    z_pass(c1, NZ // 2, 8, 1, top)
    x_pass(1, c1, NZ // 2, NXL // 2, c2, c1, 8, top)

    w_loads[2].wait()
    end = ROWS // 16
    for j in range(NJ):
        for k in range(NZ // 4):
            c2[j, pl.ds(end + 8 * k, 8), :] = c1[j, pl.ds(top + 16 * k, 8), :] * KA
    y_transform(c2, pl.ds(0, end + 32), w, 2)
    z_pass(c2, NZ // 4, NXL // 4, 2)
    z_pass(c2, NZ // 4, 8, 2, end)
    x_pass(2, c2, NZ // 4, NXL // 4, None, c2, 8, end + 4)

    def end_rate(k, carry):
        rate_copy(k, me).wait_send()
        return carry

    lax.fori_loop(1, n, end_rate, 0)


def code_kernel(c0, info, coded, dist, trial, ob, out_sem):
    group_rows = ROWS // GROUPS
    chunk = 32
    per = group_rows // chunk
    lane = lane_iota()
    step_sizes = [info[j : j + 1] for j in range(NJ)]
    squares = [jnp.zeros((8, LANES), jnp.float32)] * NJ
    for step in range(STEPS):
        trial[step] = jnp.sum(info[4:5, step : step + 1]).astype(jnp.int32)
    stores = []
    for g in range(GROUPS):
        def code_body(i, sums):
            at = pl.ds(pl.multiple_of(i * chunk, chunk), chunk)
            out = []
            for j in range(NJ):
                values = c0[j, at, :]
                inside = jnp.clip(values, -step_sizes[j], step_sizes[j])
                ob[at, pl.ds(j * LANES, LANES)] = (values - inside).astype(jnp.bfloat16)
                part = inside * inside
                acc = sums[j]
                for m in range(chunk // 8):
                    acc = acc + part[8 * m : 8 * m + 8]
                out.append(acc)
            return tuple(out)

        squares = lax.fori_loop(g * per, (g + 1) * per, code_body, tuple(squares))
        at = pl.ds(g * group_rows, group_rows)
        copy = pltpu.make_async_copy(ob.at[at], coded.at[at], out_sem.at[g])
        copy.start()
        stores.append(copy)

    result = jnp.zeros((1, 8), jnp.float32)
    column = lax.broadcasted_iota(jnp.int32, (1, 8), 1)
    for j in range(NJ):
        ratio = jnp.sum(squares[j], axis=0, keepdims=True) / (step_sizes[j] * step_sizes[j])
        for half in range(2):
            mine = (lane >= 64) if half else (lane < 64)
            mean = jnp.sum(jnp.where(mine, ratio, 0.0), axis=1, keepdims=True) / (NZ * 64 * 64)
            result = jnp.where(column == 2 * j + half, mean, result)
    dist[...] = result

    for copy in stores:
        copy.wait()


def body(snapshot, bitplanes, slopes):
    n = lax.axis_size("gx")
    vmem = pl.BlockSpec(memory_space=pltpu.VMEM)
    smem = pl.BlockSpec(memory_space=pltpu.SMEM)
    hbm = pl.BlockSpec(memory_space=pltpu.HBM)
    snapshot = pltpu.with_memory_space_constraint(snapshot.reshape(ROWS, NY), pltpu.HBM)
    matrices = pltpu.with_memory_space_constraint(jnp.asarray(y_matrices()), pltpu.HBM)
    bitplanes = pltpu.with_memory_space_constraint(bitplanes, pltpu.HBM)
    slopes = pltpu.with_memory_space_constraint(slopes.reshape(1, CANDS), pltpu.HBM)
    coeffs, info = pl.pallas_call(
        functools.partial(kernel, n),
        out_shape=(
            pltpu.VMEM((NJ, ROWS, LANES), jnp.float32),
            pltpu.VMEM((8, LANES), jnp.float32),
        ),
        in_specs=[hbm, hbm, hbm, hbm],
        out_specs=(vmem, vmem),
        scratch_shapes=[
            pltpu.VMEM((NJ, ROWS // 4 + 64, LANES), jnp.float32),
            pltpu.VMEM((NJ, ROWS // 16 + 32, LANES), jnp.float32),
            pltpu.VMEM((NJ, NZ * 16, LANES), jnp.float32),
            pltpu.VMEM((3, 2, NY, 2 * LANES), jnp.bfloat16),
            pltpu.SMEM((1, 8), jnp.int32),
            pltpu.VMEM((1, CANDS), jnp.int32),
            pltpu.VMEM((1, LANES), jnp.int32),
            pltpu.VMEM((n, 1, LANES), jnp.int32),
            *[pltpu.VMEM((6, NJ, NZ, LANES), jnp.float32)] * 4,
            pltpu.SemaphoreType.DMA((GROUPS, NJ)),
            pltpu.SemaphoreType.DMA((3,)),
            pltpu.SemaphoreType.DMA((2,)),
            pltpu.SemaphoreType.DMA((n,)),
            pltpu.SemaphoreType.DMA((n,)),
            pltpu.SemaphoreType.DMA((2,)),
            pltpu.SemaphoreType.DMA((2,)),
        ],
        compiler_params=pltpu.CompilerParams(
            collective_id=0, has_side_effects=True, vmem_limit_bytes=32 * 1024 * 1024
        ),
    )(snapshot, matrices, bitplanes, slopes)
    coded, dist, trial = pl.pallas_call(
        code_kernel,
        out_shape=(
            jax.ShapeDtypeStruct((ROWS, NY), jnp.bfloat16),
            jax.ShapeDtypeStruct((1, 8), jnp.float32),
            jax.ShapeDtypeStruct((STEPS,), jnp.int32),
        ),
        in_specs=[vmem, vmem],
        out_specs=(hbm, vmem, smem),
        scratch_shapes=[
            pltpu.VMEM((ROWS, NY), jnp.bfloat16),
            pltpu.SemaphoreType.DMA((GROUPS,)),
        ],
        compiler_params=pltpu.CompilerParams(vmem_limit_bytes=32 * 1024 * 1024),
    )(
        pltpu.with_memory_space_constraint(coeffs, pltpu.VMEM),
        pltpu.with_memory_space_constraint(info, pltpu.VMEM),
    )
    return coded.reshape(NZ, NXL, NY), dist, trial


def solution(mesh):
    return jax.shard_map(
        body,
        mesh=mesh,
        in_specs=(P(None, ("slab", "gx"), None), P(("slab", "gx"), None), P()),
        out_specs=(P(None, ("slab", "gx"), None), P(("slab", "gx"), None), P("slab")),
        check_vma=False,
    )
```

```python
import functools

import jax
import jax.numpy as jnp
import ml_dtypes
import numpy as np
from jax import lax
from jax.experimental import pallas as pl
from jax.experimental.pallas import tpu as pltpu
from jax.sharding import PartitionSpec as P

NZ, NXL, NY = 16, 64, 512
LANES = 128
NJ = NY // LANES
ROWS = NZ * NXL
CANDS = 64
STEPS = 6
GROUPS = 4
PARTS = 1

AL = -1.586134342
BE = -0.05298011854
GA = 0.8829110762
DE = 0.4435068522
KA = 1.149604398
QUANT_UNIT = 1.0 / 128.0
MESH = pl.DeviceIdType.MESH


def lane_iota(rows=1):
    return lax.broadcasted_iota(jnp.int32, (rows, LANES), 1)


def line_lift(get):
    memo = {}

    def state(kind, i):
        if (kind, i) not in memo:
            if kind == "d1":
                v = add(get(i), AL, get(i - 1), get(i + 1))
            elif kind == "s1":
                v = add(get(i), BE, state("d1", i - 1), state("d1", i + 1))
            elif kind == "d2":
                v = add(state("d1", i), GA, state("s1", i - 1), state("s1", i + 1))
            else:
                v = add(state("s1", i), DE, state("d2", i - 1), state("d2", i + 1))
            memo[kind, i] = v
        return memo[kind, i]

    return state


def add(v, weight, a, b):
    if v is None:
        return None
    both = a if b is None else b if a is None else a + b
    return v if both is None else v + weight * both


def crossing(get, before):
    if before:
        inner = add(get(-3), AL, get(-4), get(-2))
        return get(-1) + AL * get(-2), get(-2) + BE * inner
    return get(0), get(0) + BE * add(get(1), AL, get(0), get(2))


def edge_rows(row, keep):
    out, get = [], row
    for level in range(3):
        for before in (True, False):
            if keep(-1 if before else 0):
                out.append((level, before, crossing(get, before)))
        get = next_level(get, keep)
    return out


def next_level(get, keep):
    memo = {}

    def bounded(i):
        if not keep(i):
            return None
        if i not in memo:
            memo[i] = get(i)
        return memo[i]

    state = line_lift(bounded)
    return lambda k: KA * state("s2", 2 * k)


def edge_matrix():
    span = 64
    eye = np.eye(2 * span)

    def row(i):
        return eye[i + span] if -span <= i < span else np.zeros(2 * span)

    behind = edge_rows(row, lambda i: i < 0)
    ahead = edge_rows(row, lambda i: i >= 0)
    true = edge_rows(row, lambda i: True)
    given = np.stack([v for part in (behind, ahead) for _, _, pair in part for v in pair])
    wanted = [v for b in (True, False) for lv, side, pair in true if lv and side == b for v in pair]
    solved = np.linalg.lstsq(given.T, np.stack(wanted).T, rcond=None)[0].T
    assert np.abs(solved @ given - np.stack(wanted)).max() < 1e-9
    return solved


EDGES = edge_matrix()


def y_matrices():
    parts = []
    for level in range(3):
        s = 2**level
        m = np.eye(NY)
        sub = m[:, ::s].copy()
        for coefficient, first in ((AL, 1), (BE, 0), (GA, 1), (DE, 0)):
            sides = np.roll(sub, 1, 1) + np.roll(sub, -1, 1)
            sub[:, first::2] += coefficient * sides[:, first::2]
        sub[:, 0::2] *= KA
        sub[:, 1::2] /= KA
        m[:, ::s] = sub
        m = m[:, LANES : 3 * LANES].astype(np.float32)
        high = m.astype(ml_dtypes.bfloat16)
        low = (m - high.astype(np.float32)).astype(ml_dtypes.bfloat16)
        parts.append(np.stack([high, low]))
    return np.stack(parts)


def y_transform(buf, at, w, level):
    vals = [buf[j, at, :] for j in range(NJ)]
    high = [v.astype(jnp.bfloat16) for v in vals]
    low = [(v - h.astype(jnp.float32)).astype(jnp.bfloat16) for v, h in zip(vals, high)]
    rows = vals[0].shape[0]
    orders = [[(2 * half - 1 + m) % NJ for m in range(4)] for half in range(2)]

    def around(parts):
        wide = [jnp.concatenate([parts[o] for o in order], axis=1) for order in orders]
        return jnp.concatenate(wide, axis=0)

    h, l = around(high), around(low)
    out = (
        jnp.dot(h, w[level, 0], preferred_element_type=jnp.float32)
        + jnp.dot(l, w[level, 0], preferred_element_type=jnp.float32)
        + jnp.dot(h, w[level, 1], preferred_element_type=jnp.float32)
    )
    for half in range(2):
        part = out[half * rows : (half + 1) * rows]
        buf[2 * half, at, :] = part[:, :LANES]
        buf[2 * half + 1, at, :] = part[:, LANES:]


def z_pass(buf, nz, nx, level, start=0):
    def z_body(i, carry):
        at = [pl.ds(pl.multiple_of(start + k * nx + i * 8, 8), 8) for k in range(nz)]
        for j in range(NJ):
            planes = z_lift([buf[j, at[k], :] for k in range(nz)], level)
            for k in range(nz):
                buf[j, at[k], :] = planes[k]
        return carry

    lax.fori_loop(0, nx // 8, z_body, 0, unroll=True)


def weights(level):
    if level == 0:
        return AL, BE, GA, DE
    own = lane_iota() % 2**level == 0
    return tuple(jnp.where(own, c, 0.0) for c in (AL, BE, GA, DE))


def z_lift(v, level):
    n = len(v)
    w = weights(level)
    v = list(v)
    for coefficient, first in ((w[0], 1), (w[1], 0), (w[2], 1), (w[3], 0)):
        for k in range(first, n, 2):
            a = v[k - 1] if k > 0 else v[k + 1]
            b = v[k + 1] if k < n - 1 else v[k - 1]
            v[k] = v[k] + coefficient * (a + b)
    return v


def shift_up(v, last):
    rows = v.shape[0]
    index = lax.broadcasted_iota(jnp.int32, v.shape, 0)
    return jnp.where(index == rows - 1, last, pltpu.roll(v, rows - 1, 0))


def shift_down(v, first):
    index = lax.broadcasted_iota(jnp.int32, v.shape, 0)
    return jnp.where(index == 0, first, pltpu.roll(v, 1, 0))


def x_lift(even, odd, p, r, e, t, level):
    rows = even.shape[0]
    al, be, ga, de = weights(level)
    d1 = odd + al * (even + shift_up(even, e))
    d1_before = p + al * even[0:1]
    s1 = even + be * (d1 + shift_down(d1, d1_before))
    s1_before = r + be * d1_before
    s1_after = t + be * d1[rows - 1 : rows]
    d2 = d1 + ga * (s1 + shift_up(s1, s1_after))
    d2_before = d1_before + ga * (s1_before + s1[0:1])
    s2 = s1 + de * (d2 + shift_down(d2, d2_before))
    return s2, d2


def kernel(
    n, x_hbm, w_hbm, bits_hbm, slopes_hbm, c0, info,
    c1, c2, h0, w, bits, slopes, slope_row, rates,
    send_right, send_left, from_left, from_right,
    in_sem, w_sem, small_sem, rate_send, rate_recv, edge_send, edge_recv,
):
    me = lax.axis_index("gx")
    right, left = lax.rem(me + 1, n), lax.rem(me + n - 1, n)

    barrier = pltpu.get_barrier_semaphore()

    def greet(k, carry):
        pl.semaphore_signal(
            barrier, inc=1, device_id={"gx": lax.rem(me + k, n)}, device_id_type=MESH
        )
        return carry

    lax.fori_loop(1, n, greet, 0)

    group_rows = ROWS // PARTS
    loads = []
    for j in range(NJ):
        for g in range(PARTS):
            copy = pltpu.make_async_copy(
                x_hbm.at[pl.ds(g * group_rows, group_rows), pl.ds(j * LANES, LANES)],
                c0.at[j, pl.ds(g * group_rows, group_rows)],
                in_sem.at[j, g],
            )
            copy.start()
            loads.append(copy)
    small = [
        pltpu.make_async_copy(bits_hbm, bits, small_sem.at[0]),
        pltpu.make_async_copy(slopes_hbm, slopes, small_sem.at[1]),
    ]
    w_loads = [pltpu.make_async_copy(w_hbm.at[k], w.at[k], w_sem.at[k]) for k in range(3)]
    for copy in small + w_loads:
        copy.start()


    copies = []
    for j in range(NJ):
        for copy in loads[j * PARTS : (j + 1) * PARTS]:
            copy.wait()

        def row(i):
            return c0[j, pl.ds(i % NXL, NZ, stride=NXL), :]

        for level, _, pair in edge_rows(row, lambda i: i < 0):
            send_right[j, 2 * level] = pair[0]
            send_right[j, 2 * level + 1] = pair[1]
        for level, _, pair in edge_rows(row, lambda i: i >= 0):
            send_left[j, 2 * level] = pair[0]
            send_left[j, 2 * level + 1] = pair[1]
        if j == 0:
            pl.semaphore_wait(barrier, n - 1)
        for side, src, dst, to in (
            (0, send_right, from_left, right),
            (1, send_left, from_right, left),
        ):
            copy = pltpu.make_async_remote_copy(
                src_ref=src.at[j],
                dst_ref=dst.at[j],
                send_sem=edge_send.at[j, side],
                recv_sem=edge_recv.at[j, side],
                device_id={"gx": to},
                device_id_type=MESH,
            )
            copy.start()
            copies.append(copy)

    for copy in small:
        copy.wait()
    slope_row[...] = jnp.full((1, LANES), 536870911, jnp.int32)
    slope_row[:, 0:CANDS] = slopes[...]
    trial_slopes = slope_row[...]
    skipped = jnp.zeros((1, LANES), jnp.int32)
    for q in range(1, 16):
        skipped = skipped + jnp.where(trial_slopes > 4**q, 1, 0)
    own = jnp.zeros((1, LANES), jnp.int32)
    for b in range(8):
        own = own + jnp.maximum(bits[0, b] - skipped, 0)
    rates[me] = own

    def rate_copy(k, row):
        return pltpu.make_async_remote_copy(
            src_ref=rates.at[row],
            dst_ref=rates.at[row],
            send_sem=rate_send.at[k],
            recv_sem=rate_recv.at[k],
            device_id={"gx": lax.rem(me + k, n)},
            device_id_type=MESH,
        )

    def send_rate(k, carry):
        rate_copy(k, me).start()
        return carry

    lax.fori_loop(1, n, send_rate, 0)

    def x_pass(level, buf, nz, nx, nxt, edge, edge_nx, first):
        half = nx // 2
        step = 2**level
        own = lane_iota() % step == 0

        def x_body(i, carry):
            for parity in range(2):
                k = 2 * i + parity
                z_gain = 1.0 / KA if parity else KA
                even_scale, odd_scale = z_gain * KA, z_gain / KA
                if level:
                    even_scale = jnp.where(own, even_scale, 1.0)
                    odd_scale = jnp.where(own, odd_scale, 1.0)
                base = k * step * NXL
                for j in range(NJ):
                    even = buf[j, pl.ds(k * nx, half, stride=2), :]
                    odd = buf[j, pl.ds(k * nx + 1, half, stride=2), :]
                    p, r, e, t = [
                        edge[j, pl.ds(first + k * edge_nx + f, 1), :] for f in range(4)
                    ]
                    s2, d2 = x_lift(even, odd, p, r, e, t, level)
                    s2 = s2 * even_scale
                    d2 = d2 * odd_scale
                    c0[j, pl.ds(base + step, half, stride=2 * step), :] = d2
                    if parity == 0 and level < 2:
                        nxt[j, pl.ds(pl.multiple_of(i * half, 8), half), :] = s2
                    else:
                        c0[j, pl.ds(base, half, stride=2 * step), :] = s2
            return carry

        lax.fori_loop(0, nz // 2, x_body, 0, unroll=min(4, nz // 2))

    w_loads[0].wait()

    def y_body(i, carry):
        y_transform(c0, pl.ds(pl.multiple_of(i * 256, 256), 256), w, 0)
        return carry

    lax.fori_loop(0, ROWS // 256, y_body, 0)
    z_pass(c0, NZ, NXL, 0)

    def take_rate(k, carry):
        rate_copy(k, lax.rem(me - k + n, n)).wait_recv()
        return carry

    lax.fori_loop(1, n, take_rate, 0)
    total = jnp.sum(rates[...], axis=0)
    lane = lane_iota()
    target = 2 * 8 * n
    total_f = total.astype(jnp.float32)
    over = jnp.where((lane < CANDS - 1) & (total > target), 1.0, 0.0)
    lower = jnp.sum(over, axis=1, keepdims=True).astype(jnp.int32)
    found = jnp.zeros((1, LANES), jnp.float32)
    for step in range(STEPS):
        span = 2 ** (STEPS - step)
        middle = (lower & (64 - span)) + (span // 2 - 1)
        picked = jnp.sum(jnp.where(lane == middle, total_f, 0.0), axis=1, keepdims=True)
        found = jnp.where(lane == step, picked, found)
    skip = jnp.sum(
        jnp.where(lane == lower, skipped.astype(jnp.float32), 0.0), axis=1, keepdims=True
    ).astype(jnp.int32)
    for j in range(NJ):
        planes = jnp.minimum(jnp.where(lane < 64, bits[0, 2 * j], bits[0, 2 * j + 1]), skip)
        info[j : j + 1] = QUANT_UNIT * jnp.left_shift(jnp.int32(1), planes).astype(jnp.float32)
    info[4:5] = found

    def cross_rows(j):
        mine_right = [send_right[j, f] for f in range(6)]
        mine_left = [send_left[j, f] for f in range(6)]
        theirs_left = [from_left[j, f] for f in range(6)]
        theirs_right = [from_right[j, f] for f in range(6)]

        def put(f, v):
            h0[j, pl.ds(f, NZ, stride=16), :] = v

        put(0, theirs_left[0])
        put(1, theirs_left[1])
        put(2, theirs_right[0])
        put(3, theirs_right[1])
        for f in range(4, 8):
            put(f, jnp.zeros((NZ, LANES), jnp.float32))
        for side, given in ((0, theirs_left + mine_left), (1, mine_right + theirs_right)):
            for f in range(4):
                total = None
                for c, v in zip(EDGES[4 * side + f], given):
                    if abs(c) > 1e-12:
                        total = float(c) * v if total is None else total + float(c) * v
                put(8 + 4 * (f // 2) + 2 * side + f % 2, total)

    for j in range(NJ):
        copies[2 * j].wait()
        copies[2 * j + 1].wait()
        cross_rows(j)
    y_transform(h0, pl.ds(0, 256), w, 0)
    z_pass(h0, NZ, 16, 0)
    x_pass(0, c0, NZ, NXL, c1, h0, 16, 0)

    w_loads[1].wait()
    top = ROWS // 4
    for j in range(NJ):
        for k in range(NZ // 2):
            c1[j, pl.ds(top + 8 * k, 8), :] = h0[j, pl.ds(32 * k + 8, 8), :] * KA
    y_transform(c1, pl.ds(0, top + 64), w, 1)
    z_pass(c1, NZ // 2, NXL // 2, 1)
    z_pass(c1, NZ // 2, 8, 1, top)
    x_pass(1, c1, NZ // 2, NXL // 2, c2, c1, 8, top)

    w_loads[2].wait()
    end = ROWS // 16
    for j in range(NJ):
        for k in range(NZ // 4):
            c2[j, pl.ds(end + 8 * k, 8), :] = c1[j, pl.ds(top + 16 * k, 8), :] * KA
    y_transform(c2, pl.ds(0, end + 32), w, 2)
    z_pass(c2, NZ // 4, NXL // 4, 2)
    z_pass(c2, NZ // 4, 8, 2, end)
    x_pass(2, c2, NZ // 4, NXL // 4, None, c2, 8, end + 4)

    def end_rate(k, carry):
        rate_copy(k, me).wait_send()
        return carry

    lax.fori_loop(1, n, end_rate, 0)


def code_kernel(c0, info, coded, dist, trial, ob, out_sem):
    group_rows = ROWS // GROUPS
    chunk = 32
    per = group_rows // chunk
    lane = lane_iota()
    step_sizes = [info[j : j + 1] for j in range(NJ)]
    squares = [jnp.zeros((8, LANES), jnp.float32)] * NJ
    for step in range(STEPS):
        trial[step] = jnp.sum(info[4:5, step : step + 1]).astype(jnp.int32)
    stores = []
    for g in range(GROUPS):
        def code_body(i, sums):
            at = pl.ds(pl.multiple_of(i * chunk, chunk), chunk)
            out = []
            for j in range(NJ):
                values = c0[j, at, :]
                inside = jnp.clip(values, -step_sizes[j], step_sizes[j])
                ob[at, pl.ds(j * LANES, LANES)] = (values - inside).astype(jnp.bfloat16)
                part = inside * inside
                acc = sums[j]
                for m in range(chunk // 8):
                    acc = acc + part[8 * m : 8 * m + 8]
                out.append(acc)
            return tuple(out)

        squares = lax.fori_loop(g * per, (g + 1) * per, code_body, tuple(squares))
        at = pl.ds(g * group_rows, group_rows)
        copy = pltpu.make_async_copy(ob.at[at], coded.at[at], out_sem.at[g])
        copy.start()
        stores.append(copy)

    result = jnp.zeros((1, 8), jnp.float32)
    column = lax.broadcasted_iota(jnp.int32, (1, 8), 1)
    for j in range(NJ):
        ratio = jnp.sum(squares[j], axis=0, keepdims=True) / (step_sizes[j] * step_sizes[j])
        for half in range(2):
            mine = (lane >= 64) if half else (lane < 64)
            mean = jnp.sum(jnp.where(mine, ratio, 0.0), axis=1, keepdims=True) / (NZ * 64 * 64)
            result = jnp.where(column == 2 * j + half, mean, result)
    dist[...] = result

    for copy in stores:
        copy.wait()


def body(snapshot, bitplanes, slopes):
    n = lax.axis_size("gx")
    vmem = pl.BlockSpec(memory_space=pltpu.VMEM)
    smem = pl.BlockSpec(memory_space=pltpu.SMEM)
    hbm = pl.BlockSpec(memory_space=pltpu.HBM)
    snapshot = pltpu.with_memory_space_constraint(snapshot.reshape(ROWS, NY), pltpu.HBM)
    matrices = pltpu.with_memory_space_constraint(jnp.asarray(y_matrices()), pltpu.HBM)
    bitplanes = pltpu.with_memory_space_constraint(bitplanes, pltpu.HBM)
    slopes = pltpu.with_memory_space_constraint(slopes.reshape(1, CANDS), pltpu.HBM)
    coeffs, info = pl.pallas_call(
        functools.partial(kernel, n),
        out_shape=(
            pltpu.VMEM((NJ, ROWS, LANES), jnp.float32),
            pltpu.VMEM((8, LANES), jnp.float32),
        ),
        in_specs=[hbm, hbm, hbm, hbm],
        out_specs=(vmem, vmem),
        scratch_shapes=[
            pltpu.VMEM((NJ, ROWS // 4 + 64, LANES), jnp.float32),
            pltpu.VMEM((NJ, ROWS // 16 + 32, LANES), jnp.float32),
            pltpu.VMEM((NJ, NZ * 16, LANES), jnp.float32),
            pltpu.VMEM((3, 2, NY, 2 * LANES), jnp.bfloat16),
            pltpu.SMEM((1, 8), jnp.int32),
            pltpu.VMEM((1, CANDS), jnp.int32),
            pltpu.VMEM((1, LANES), jnp.int32),
            pltpu.VMEM((n, 1, LANES), jnp.int32),
            *[pltpu.VMEM((NJ, 6, NZ, LANES), jnp.float32)] * 4,
            pltpu.SemaphoreType.DMA((NJ, PARTS)),
            pltpu.SemaphoreType.DMA((3,)),
            pltpu.SemaphoreType.DMA((2,)),
            pltpu.SemaphoreType.DMA((n,)),
            pltpu.SemaphoreType.DMA((n,)),
            pltpu.SemaphoreType.DMA((NJ, 2)),
            pltpu.SemaphoreType.DMA((NJ, 2)),
        ],
        compiler_params=pltpu.CompilerParams(
            collective_id=0, has_side_effects=True, vmem_limit_bytes=32 * 1024 * 1024
        ),
    )(snapshot, matrices, bitplanes, slopes)
    coded, dist, trial = pl.pallas_call(
        code_kernel,
        out_shape=(
            jax.ShapeDtypeStruct((ROWS, NY), jnp.bfloat16),
            jax.ShapeDtypeStruct((1, 8), jnp.float32),
            jax.ShapeDtypeStruct((STEPS,), jnp.int32),
        ),
        in_specs=[vmem, vmem],
        out_specs=(hbm, vmem, smem),
        scratch_shapes=[
            pltpu.VMEM((ROWS, NY), jnp.bfloat16),
            pltpu.SemaphoreType.DMA((GROUPS,)),
        ],
        compiler_params=pltpu.CompilerParams(vmem_limit_bytes=32 * 1024 * 1024),
    )(
        pltpu.with_memory_space_constraint(coeffs, pltpu.VMEM),
        pltpu.with_memory_space_constraint(info, pltpu.VMEM),
    )
    return coded.reshape(NZ, NXL, NY), dist, trial


def solution(mesh):
    return jax.shard_map(
        body,
        mesh=mesh,
        in_specs=(P(None, ("slab", "gx"), None), P(("slab", "gx"), None), P()),
        out_specs=(P(None, ("slab", "gx"), None), P(("slab", "gx"), None), P("slab")),
        check_vma=False,
    )
```
